512 devices in a mesh: blk: 16 (over x_lo, y), grp: 32 (over z, x_hi, core).
Axes of the slice: x: 4 (x_hi: 2, x_lo: 2; x = x_hi * 2 + x_lo), y: 8, z: 8, core: 2. Of those that a mesh axis runs over, the one named last changes fastest.
Arguments:
- own_tiles: bfloat16 [61440, 128, 128], P(('blk', 'grp')), may hold values from 4 to 24865, as said below
- own_rows: int32 [61440], P(('blk', 'grp')), may hold values from 0 to 31
- own_cols: int32 [61440], P(('blk', 'grp')), may hold values from 0 to 15
- hub_tiles: bfloat16 [8192, 1, 128, 128], P(('blk', 'grp')), may hold values from 4 to 24865, as said below
- hub_rows: int32 [8192, 1], P(('blk', 'grp')), may hold values from 0 to 31
- hub_cols: int32 [8192, 1], P(('blk', 'grp')), may hold values from 0 to 15
- factor: float32 [65536, 128], P(('blk', 'grp')), may hold values from 0.001 to 25, as said below
Outputs:
- updated: float32 [65536, 128], P(('blk', 'grp'))
The draws below stay inside these ranges and needn't reach their ends.
Inputs may be any that keep to these rules, and one draw needn't show every extreme that they name: `hub_rows`: every device holds exactly 120 own tiles and 1 hub tiles for each index of blk; tiles may share coordinates, and then they add. `factor`: every entry is positive. `own_tiles`: every entry is positive. `hub_tiles`: every entry is positive.
All inputs are finite; a program needn't handle non-finite values.
Results may differ from the reference program's by a relative error of at most 0.0015.
Values may be sent and summed in bfloat16 or wider, within the bound.
A program may use at most 64 MiB of HBM per device.

```python
import math
import jax
import jax.numpy as jnp
import numpy as np
from jax import lax

RANK = 128
TILE = 128
ROWS_DEV = 128
TILE_DEV = 120
HUB = 1
ITERS = 2
SEGMENTS = 512
NROWS = 65536
ROW_TILES = 32
COL_TILES = 16
N_BLK = 16
N_GRP = 32


def boost_pattern(key):
    key = jax.random.fold_in(key, 97)
    ordering = jax.random.permutation(key, TILE)
    matches = (ordering[:, None] == jnp.arange(TILE)[None, :]).astype(jnp.float32)
    return 1.0 + TILE * matches


def tile_scale():
    return 0.075 * NROWS * RANK * ROWS_DEV / ((TILE_DEV + N_BLK * HUB) * TILE * TILE)


def draw_own_tiles(key, part):
    pattern = boost_pattern(key)
    key = jax.random.fold_in(key, 5)
    tile_shape = (SEGMENTS * TILE_DEV, TILE, TILE)
    jitter = jnp.exp(jax.random.uniform(key, tile_shape, jnp.float32, math.log(0.25), math.log(4.0)))
    return (tile_scale() * jitter * pattern).astype(jnp.bfloat16)


def draw_hub_tiles(key, part):
    pattern = boost_pattern(key)
    key = jax.random.fold_in(key, 7)
    tile_shape = (SEGMENTS * N_BLK, HUB, TILE, TILE)
    jitter = jnp.exp(jax.random.uniform(key, tile_shape, jnp.float32, math.log(0.25), math.log(4.0)))
    return (tile_scale() * jitter * pattern).astype(jnp.bfloat16)


def draw_factor(key, part):
    key = jax.random.fold_in(key, 11)
    k_row = jax.random.fold_in(key, 0)
    k_col = jax.random.fold_in(key, 1)
    k_ent = jax.random.fold_in(key, 2)
    k_pos = jax.random.fold_in(key, 4)
    segment = (jnp.arange(NROWS) // ROWS_DEV).astype(jnp.float32)
    growth = 1.0 + 0.75 * segment / (SEGMENTS - 1)
    row_scale = jnp.exp(jax.random.uniform(k_row, (NROWS, 1), jnp.float32, math.log(0.2), math.log(2.0)))
    col_scale = jnp.exp(jax.random.uniform(k_col, (1, RANK), jnp.float32, math.log(0.2), math.log(2.0)))
    profile = jnp.exp(jax.random.uniform(k_pos, (TILE, RANK), jnp.float32, math.log(0.05), math.log(1.0)))
    position_part = jnp.tile(profile, (NROWS // TILE, 1))
    entries = jnp.exp(jax.random.uniform(k_ent, (NROWS, RANK), jnp.float32, math.log(0.5), math.log(2.0)))
    return row_scale * col_scale * entries * position_part * growth[:, None]


def place_ends(values, own_key, low, top_value):
    longest = values.shape.index(max(values.shape))
    spots = []
    for shift in (0, 1):
        where = [jax.random.randint(jax.random.fold_in(own_key, axis), (), 0, length) for axis, length in enumerate(values.shape)]
        where[longest] = (where[longest] + shift) % values.shape[longest]
        spots.append(tuple(where))
    return values.at[spots[0]].set(low).at[spots[1]].set(top_value)


def cumulative_ranks(number_of, skew):
    portions = [(1 << 20) // math.isqrt(rank ** skew) + 1 for rank in range(1, number_of + 1)]
    scale = 1 + sum(portions) // (1 << 30)
    return np.cumsum(np.array([max(1, weight // scale) for weight in portions]))


def ranked(rng, dims, count, slope):
    listing = cumulative_ranks(count, slope)
    lot = jax.random.randint(jax.random.fold_in(rng, 1), dims, 0, int(listing[count - 1]))
    rank = jnp.searchsorted(jnp.asarray(listing, jnp.int32), lot, side="right")
    return jax.random.permutation(jax.random.fold_in(rng, 2), count)[rank].astype(jnp.int32)


def setup_inputs(seed: int = 0) -> dict:
    splits = jax.random.split(jax.random.key(seed), 8)
    own_tiles = draw_own_tiles(jax.random.fold_in(splits[7], 71), 0)
    own_rows = place_ends(jax.random.randint(splits[1], (SEGMENTS * TILE_DEV,), 0, ROW_TILES), jax.random.fold_in(splits[1], 1), 0, ROW_TILES - 1).astype(jnp.int32)
    own_cols = place_ends(jax.random.randint(splits[2], (SEGMENTS * TILE_DEV,), 0, COL_TILES), jax.random.fold_in(splits[2], 1), 0, COL_TILES - 1).astype(jnp.int32)
    hub_tiles = draw_hub_tiles(jax.random.fold_in(splits[7], 71), 0)
    hub_rows = place_ends(ranked(splits[4], (SEGMENTS * N_BLK, HUB), ROW_TILES, 2), jax.random.fold_in(splits[4], 3), 0, ROW_TILES - 1).astype(jnp.int32)
    hub_cols = place_ends(jax.random.randint(splits[5], (SEGMENTS * N_BLK, HUB), 0, COL_TILES), jax.random.fold_in(splits[5], 1), 0, COL_TILES - 1).astype(jnp.int32)
    factor = draw_factor(jax.random.fold_in(splits[7], 71), 0)
    return dict(own_tiles=own_tiles, own_rows=own_rows, own_cols=own_cols, hub_tiles=hub_tiles, hub_rows=hub_rows, hub_cols=hub_cols, factor=factor)


damping = 0.5


def block_image(b_index, g_index, own_tiles, own_rows, own_cols, hub_tiles, hub_rows, hub_cols, low_factor):
    segment = (b_index * N_GRP + g_index).astype(jnp.int32)
    grid = low_factor.reshape(N_BLK, N_GRP, ROWS_DEV, RANK)
    column_rows = lax.dynamic_index_in_dim(grid, g_index.astype(jnp.int32), 1, keepdims=False)
    col_blocks = column_rows.reshape(COL_TILES, TILE, RANK).astype(jnp.float32)
    mine = lax.dynamic_index_in_dim(own_tiles.reshape(SEGMENTS, TILE_DEV, TILE, TILE), segment, 0, keepdims=False)
    mine_rows = lax.dynamic_index_in_dim(own_rows.reshape(SEGMENTS, TILE_DEV), segment, 0, keepdims=False)
    mine_cols = lax.dynamic_index_in_dim(own_cols.reshape(SEGMENTS, TILE_DEV), segment, 0, keepdims=False)
    hub_grid = hub_tiles.reshape(N_BLK, N_GRP, N_BLK, HUB, TILE, TILE)
    hub_group = lax.dynamic_index_in_dim(hub_grid, g_index.astype(jnp.int32), 1, keepdims=False)
    incoming = lax.dynamic_index_in_dim(hub_group, b_index.astype(jnp.int32), 1, keepdims=False)
    in_rows = lax.dynamic_index_in_dim(lax.dynamic_index_in_dim(hub_rows.reshape(N_BLK, N_GRP, N_BLK, HUB), g_index.astype(jnp.int32), 1, keepdims=False), b_index.astype(jnp.int32), 1, keepdims=False)
    in_cols = lax.dynamic_index_in_dim(lax.dynamic_index_in_dim(hub_cols.reshape(N_BLK, N_GRP, N_BLK, HUB), g_index.astype(jnp.int32), 1, keepdims=False), b_index.astype(jnp.int32), 1, keepdims=False)
    all_tiles = jnp.concatenate([mine, incoming.reshape(N_BLK * HUB, TILE, TILE)], axis=0).astype(jnp.float32)
    all_rows = jnp.concatenate([mine_rows, in_rows.reshape(N_BLK * HUB)], axis=0).astype(jnp.int32)
    all_cols = jnp.concatenate([mine_cols, in_cols.reshape(N_BLK * HUB)], axis=0).astype(jnp.int32)
    products = jnp.einsum("tij,tjk->tik", all_tiles, col_blocks[all_cols])
    summed = jax.ops.segment_sum(products, all_rows, num_segments=ROW_TILES)
    return summed.reshape(N_GRP * ROWS_DEV, RANK)


def reference(own_tiles, own_rows, own_cols, hub_tiles, hub_rows, hub_cols, factor):
    current = factor
    for sweep in range(ITERS):
        low_factor = current.astype(jnp.bfloat16)
        gram_matrix = jnp.dot(low_factor.T, low_factor, preferred_element_type=jnp.float32)

        def row_block(b_index):
            def add_group(total, g_index):
                part_sum = block_image(b_index, g_index, own_tiles, own_rows, own_cols, hub_tiles, hub_rows, hub_cols, low_factor)
                return total + part_sum, None

            start = jnp.zeros((N_GRP * ROWS_DEV, RANK), jnp.float32)
            total, unused = lax.scan(add_group, start, jnp.arange(N_GRP, dtype=jnp.int32))
            return total

        product_rows = lax.map(row_block, jnp.arange(N_BLK, dtype=jnp.int32)).reshape(NROWS, RANK)
        curvature = jnp.dot(current, gram_matrix, precision=lax.Precision.HIGHEST)
        current = current * (1.0 - damping + damping * product_rows / curvature)
    return current
```

```python
import jax
import jax.numpy as jnp
from jax import lax
from jax.experimental import pallas as pl
from jax.experimental.pallas import tpu as pltpu
from jax.sharding import PartitionSpec as P

ITERS = 2
T = 128
NB = 16
NG = 32
NZ = 8
OWN = 120
MESH = pl.DeviceIdType.MESH
damping = 0.5

RING = (4, 3, 5, 2, 6, 1, 7)
BLK_ORDER = tuple((h, k) for k in (4, 3, 5, 2, 6, 1, 7) for h in (1, 0)) + ((1, 0),)


def kernel(own_hbm, own_rows, own_cols, hub_hbm, hub_rows, hub_cols, factor, out,
           own_v, hub_v, meta, meta_in, gath0, gath1, acc, ptr_v, ptr_s,
           send_a, send_b, send_c, recv_a0, recv_a1, recv_b0, recv_b1, recv_c0, recv_c1,
           gram_own, gram_in0, gram_in1, gram0, gram1,
           local_sem, ptr_sem, meta_ssem, meta_rsem, hub_ssem, hub_rsem,
           ag_ssem, ag_rsem, a_ssem, a_rsem, b_ssem, b_rsem, c_ssem, c_rsem,
           g_ssem, g_rsem, h_ssem, h_rsem):
    b, g = lax.axis_index("blk"), lax.axis_index("grp")
    y = lax.rem(b, NZ)
    half = b // NZ
    c = lax.rem(g, 2)
    xh = lax.rem(g, 4) // 2
    z = g // 4

    def blk_peer(h, k):
        return lax.rem(half + h, 2) * NZ + lax.rem(y + k, NZ)

    def wait(like, sem):
        pltpu.make_async_copy(like, like, sem).wait()

    tiles_copy = pltpu.make_async_copy(own_hbm, own_v, local_sem.at[0])
    tiles_copy.start()
    hub_copy = pltpu.make_async_copy(hub_hbm.at[b], hub_v.at[b], local_sem.at[1])
    hub_copy.start()

    barrier = pltpu.get_barrier_semaphore()
    for h, k in BLK_ORDER:
        pl.semaphore_signal(barrier, inc=1, device_id=(blk_peer(h, k), g), device_id_type=MESH)

    def greet(k, _):
        pl.semaphore_signal(barrier, inc=1, device_id=(b, lax.rem(g + k, NG)), device_id_type=MESH)
        return 0

    lax.fori_loop(1, NG, greet, 0)

    for d in range(NB):
        meta[d] = jnp.full((8, T), hub_rows[d, 0] * NB + hub_cols[d, 0], jnp.int32)
    acc[0] = jnp.zeros((T, T), jnp.float32)
    low = factor[...].astype(jnp.bfloat16)
    gath0[b] = low

    pl.semaphore_wait(barrier, NB - 1 + NG - 1)

    def send_factor(gath, sweep):
        for h, k in BLK_ORDER:
            pltpu.make_async_remote_copy(
                gath.at[b], gath.at[b], ag_ssem.at[sweep], ag_rsem.at[sweep],
                device_id=(blk_peer(h, k), g), device_id_type=MESH).start()

    for h, k in BLK_ORDER:
        d = blk_peer(h, k)
        pltpu.make_async_remote_copy(
            meta.at[d], meta_in.at[b], meta_ssem, meta_rsem, device_id=(d, g), device_id_type=MESH).start()
    send_factor(gath0, 0)
    for h, k in BLK_ORDER:
        d = blk_peer(h, k)
        pltpu.make_async_remote_copy(
            hub_hbm.at[d], hub_v.at[b], hub_ssem, hub_rsem, device_id=(d, g), device_id_type=MESH).start()
    meta_in[b] = meta[b]

    lane = lax.broadcasted_iota(jnp.int32, (8, T), 1)
    sub = lax.broadcasted_iota(jnp.int32, (8, T), 0)

    def lay(u, rows):
        return jnp.where(lane == u, own_rows[u], rows)

    rows = lax.fori_loop(0, OWN, lay, jnp.full((8, T), -1, jnp.int32), unroll=8)
    wait(meta_in.at[pl.ds(0, NB - 1)], meta_rsem)
    hub_r = jnp.full((8, T), -1, jnp.int32)
    hub_c = jnp.zeros((8, T), jnp.int32)
    for e in range(NB):
        v = meta_in[e]
        hub_r = jnp.where(lane == e, v // NB, hub_r)
        hub_c = jnp.where(lane == e, lax.rem(v, NB), hub_c)

    def chain(u, state):
        prev_o, prev_h, last = state
        r = own_rows[u]
        prev_o = jnp.where((rows == r) & (lane > u), u + 1, prev_o)
        prev_h = jnp.where(hub_r == r, u + 1, prev_h)
        last = jnp.where(lane == r, u + 1, last)
        return prev_o, prev_h, last

    zeros = jnp.zeros((8, T), jnp.int32)
    prev_o, prev_h, last = lax.fori_loop(0, OWN, chain, (zeros, zeros, zeros), unroll=8)
    for e in range(NB):
        r = meta_in[e] // NB
        prev_h = jnp.where((hub_r == r) & (lane > e), OWN + e + 1, prev_h)
        last = jnp.where(lane == r, OWN + e + 1, last)
    ptr_v[...] = jnp.where(sub == 0, prev_o, jnp.where(sub == 1, prev_h, jnp.where(sub == 2, last, hub_c)))
    ptr_copy = pltpu.make_async_copy(ptr_v, ptr_s, ptr_sem)
    ptr_copy.start()
    ptr_copy.wait()

    def row_sum(zz, hh, cc):
        return acc[ptr_s[2, zz * 4 + hh * 2 + cc]]

    current = factor[...]
    for sweep in range(ITERS):
        gath, recv_a, recv_b, recv_c, gram_in, gram = (
            (gath0, recv_a0, recv_b0, recv_c0, gram_in0, gram0),
            (gath1, recv_a1, recv_b1, recv_c1, gram_in1, gram1),
        )[sweep]
        if sweep:
            gath[b] = current.astype(jnp.bfloat16)
            send_factor(gath, sweep)
        wait(gath.at[pl.ds(0, NB - 1)], ag_rsem.at[sweep])

        every = gath[...].reshape(NB * T, T)
        group = lax.dot_general(every, every, (((0,), (0,)), ((), ())), preferred_element_type=jnp.float32)
        if sweep:
            wait(gram_in0.at[pl.ds(0, NG - 1)], g_ssem.at[0])
        gram_own[...] = group.reshape(NB, 8, T)

        def send_gram(k, _):
            pltpu.make_async_remote_copy(
                gram_own.at[b], gram_in.at[g], g_ssem.at[sweep], g_rsem.at[sweep],
                device_id=(b, lax.rem(g + k, NG)), device_id_type=MESH).start()
            return 0

        lax.fori_loop(1, NG, send_gram, 0)
        gram_in[g] = gram_own[b]

        if sweep == 0:
            tiles_copy.wait()

        def own_step(t, _):
            p = jnp.dot(own_v[t], gath[own_cols[t]], preferred_element_type=jnp.float32)
            acc[t + 1] = acc[ptr_s[0, t]] + p
            return 0

        lax.fori_loop(0, OWN, own_step, 0, unroll=8)

        wait(gram_in.at[pl.ds(0, NG - 1)], g_rsem.at[sweep])
        gram[b] = jnp.sum(gram_in[...], axis=0)
        for h, k in BLK_ORDER:
            pltpu.make_async_remote_copy(
                gram.at[b], gram.at[b], h_ssem.at[sweep], h_rsem.at[sweep],
                device_id=(blk_peer(h, k), g), device_id_type=MESH).start()

        if sweep == 0:
            hub_copy.wait()
            wait(hub_v.at[pl.ds(0, NB - 1)], hub_rsem)

        def hub_step(t, _):
            p = jnp.dot(hub_v[t], gath[ptr_s[3, t]], preferred_element_type=jnp.float32)
            acc[OWN + t + 1] = acc[ptr_s[1, t]] + p
            return 0

        lax.fori_loop(0, NB, hub_step, 0, unroll=8)

        if sweep:
            wait(send_a, a_ssem)
            wait(send_b, b_ssem)
            wait(send_c.at[pl.ds(0, NZ - 1)], c_ssem)
        for j in range(2):
            hh = lax.rem(xh + 1 + j, 2)

            def lay_a(k, _):
                send_a[j * NZ + k] = row_sum(k, hh, 1 - c).astype(jnp.bfloat16)
                return 0

            lax.fori_loop(0, NZ, lay_a, 0, unroll=4)
            part = pl.ds(j * NZ, NZ)
            pltpu.make_async_remote_copy(
                send_a.at[part], recv_a.at[part], a_ssem, a_rsem.at[sweep, j],
                device_id=(b, g + 1 - 2 * c), device_id_type=MESH).start()
        wait(recv_a.at[pl.ds(0, NZ)], a_rsem.at[sweep, 0])
        for k in RING + (0,):
            zz = lax.rem(z + k, NZ)
            send_b[zz] = (row_sum(zz, 1 - xh, c) + recv_a[zz].astype(jnp.float32)).astype(jnp.bfloat16)
            pltpu.make_async_remote_copy(
                send_b.at[zz], recv_b.at[zz], b_ssem, b_rsem.at[sweep, zz],
                device_id=(b, g + 2 - 4 * xh), device_id_type=MESH).start()
        wait(recv_a.at[pl.ds(NZ, NZ)], a_rsem.at[sweep, 1])
        total = None
        for k in RING + (0,):
            zz = lax.rem(z + k, NZ)
            mine = row_sum(zz, xh, c) + recv_a[NZ + zz].astype(jnp.float32)
            wait(recv_b.at[zz], b_rsem.at[sweep, zz])
            total = mine + recv_b[zz].astype(jnp.float32)
            if k:
                send_c[zz] = total.astype(jnp.bfloat16)
                pltpu.make_async_remote_copy(
                    send_c.at[zz], recv_c.at[z], c_ssem, c_rsem.at[sweep],
                    device_id=(b, zz * 4 + xh * 2 + c), device_id_type=MESH).start()

        wait(gram.at[pl.ds(0, NB - 1)], h_rsem.at[sweep])
        curvature = jnp.dot(current, gram[...].reshape(T, T), precision=lax.Precision.HIGHEST,
                            preferred_element_type=jnp.float32)
        wait(recv_c.at[pl.ds(0, NZ - 1)], c_rsem.at[sweep])
        for k in RING:
            total = total + recv_c[lax.rem(z + k, NZ)].astype(jnp.float32)
        current = current * (1.0 - damping + damping * total / curvature)

    out[...] = current
    wait(meta_in.at[pl.ds(0, NB - 1)], meta_ssem)
    wait(hub_v.at[pl.ds(0, NB - 1)], hub_ssem)
    wait(gram_in1.at[pl.ds(0, NG - 1)], g_ssem.at[1])
    for sweep in range(ITERS):
        wait(gath0.at[pl.ds(0, NB - 1)], ag_ssem.at[sweep])
        wait(gram0.at[pl.ds(0, NB - 1)], h_ssem.at[sweep])
    wait(send_a, a_ssem)
    wait(send_b, b_ssem)
    wait(send_c.at[pl.ds(0, NZ - 1)], c_ssem)


def body(own_tiles, own_rows, own_cols, hub_tiles, hub_rows, hub_cols, factor):
    bf, f32, i32 = jnp.bfloat16, jnp.float32, jnp.int32
    V, S, D = pltpu.VMEM, pltpu.SMEM, pltpu.SemaphoreType.DMA
    vmem, smem, hbm = (pl.BlockSpec(memory_space=m) for m in (V, S, pl.ANY))
    return pl.pallas_call(
        kernel,
        out_shape=jax.ShapeDtypeStruct((T, T), f32),
        in_specs=[hbm, smem, smem, hbm, smem, smem, vmem],
        out_specs=vmem,
        scratch_shapes=[
            V((OWN, T, T), bf), V((NB, T, T), bf), V((NB, 8, T), i32), V((NB, 8, T), i32),
            V((NB, T, T), bf), V((NB, T, T), bf), V((OWN + NB + 1, T, T), f32), V((8, T), i32), S((8, T), i32),
            V((2 * NZ, T, T), bf), V((NZ, T, T), bf), V((NZ, T, T), bf),
            V((2 * NZ, T, T), bf), V((2 * NZ, T, T), bf), V((NZ, T, T), bf), V((NZ, T, T), bf),
            V((NZ, T, T), bf), V((NZ, T, T), bf),
            V((NB, 8, T), f32), V((NG, 8, T), f32), V((NG, 8, T), f32), V((NB, 8, T), f32), V((NB, 8, T), f32),
            D((2,)), D, D, D, D, D,
            D((2,)), D((2,)), D, D((2, 2)), D, D((2, NZ)), D, D((2,)),
            D((2,)), D((2,)), D((2,)), D((2,)),
        ],
        compiler_params=pltpu.CompilerParams(
            collective_id=1, has_side_effects=True, vmem_limit_bytes=48 << 20),
    )(own_tiles, own_rows, own_cols, hub_tiles.reshape(NB, T, T), hub_rows, hub_cols, factor)


def solution(mesh):
    in_specs = (
        P(("blk", "grp"), None, None),
        P(("blk", "grp")),
        P(("blk", "grp")),
        P(("blk", "grp"), None, None, None),
        P(("blk", "grp"), None),
        P(("blk", "grp"), None),
        P(("blk", "grp"), None),
    )
    out_specs = P(("blk", "grp"), None)
    return jax.shard_map(body, mesh=mesh, in_specs=in_specs, out_specs=out_specs, check_vma=False)
```

```python
import jax
import jax.numpy as jnp
from jax import lax
from jax.experimental import pallas as pl
from jax.experimental.pallas import tpu as pltpu
from jax.sharding import PartitionSpec as P

ITERS = 2
T = 128
NB = 16
NG = 32
NZ = 8
OWN = 120
MESH = pl.DeviceIdType.MESH
damping = 0.5

RING = (4, 3, 5, 2, 6, 1, 7)
BLK_ORDER = tuple((h, k) for k in (4, 3, 5, 2, 6, 1, 7) for h in (1, 0)) + ((1, 0),)


def kernel(own_hbm, own_rows_hbm, own_cols_hbm, hub_hbm, hub_rows_hbm, hub_cols_hbm, factor_hbm, out,
           own_rows, own_cols, hub_rows, hub_cols, factor, own_v, hub_v, meta, meta_in, gath0, gath1, acc, ptr_v, ptr_s,
           send_a, send_b, send_c, recv_a0, recv_a1, recv_b0, recv_b1, recv_c0, recv_c1,
           gram_own0, gram_own1, blk_in0, blk_in1, quad_in0, quad_in1, z_in0, z_in1, gram0, gram1,
           local_sem, ptr_sem, meta_ssem, meta_rsem, hub_ssem, hub_rsem,
           ag_ssem, ag_rsem, a_ssem, a_rsem, b_ssem, b_rsem, c_ssem, c_rsem,
           gb_ssem, gb_rsem, gq_ssem, gq_rsem, gz_ssem, gz_rsem, h_ssem, h_rsem):
    b, g = lax.axis_index("blk"), lax.axis_index("grp")
    y = lax.rem(b, NZ)
    half = b // NZ
    c = lax.rem(g, 2)
    xh = lax.rem(g, 4) // 2
    z = g // 4

    def blk_peer(h, k):
        return lax.rem(half + h, 2) * NZ + lax.rem(y + k, NZ)

    def quad(k):
        return g // 4 * 4 + lax.rem(g + k, 4)

    def z_peer(k):
        return lax.rem(g + 4 * k, NG)

    def wait(like, sem):
        pltpu.make_async_copy(like, like, sem).wait()

    small = [
        pltpu.make_async_copy(src, dst, local_sem.at[2 + i])
        for i, (src, dst) in enumerate((
            (factor_hbm, factor), (hub_rows_hbm, hub_rows), (hub_cols_hbm, hub_cols),
            (own_rows_hbm, own_rows), (own_cols_hbm, own_cols)))
    ]
    for copy in small:
        copy.start()
    tiles_copy = pltpu.make_async_copy(own_hbm, own_v, local_sem.at[0])
    tiles_copy.start()
    hub_copy = pltpu.make_async_copy(hub_hbm.at[b], hub_v.at[b], local_sem.at[1])
    hub_copy.start()

    barrier = pltpu.get_barrier_semaphore()
    for h, k in BLK_ORDER:
        pl.semaphore_signal(barrier, inc=1, device_id=(blk_peer(h, k), g), device_id_type=MESH)

    for k in (1, 2, 3):
        pl.semaphore_signal(barrier, inc=1, device_id=(b, quad(k)), device_id_type=MESH)
    for k in RING:
        pl.semaphore_signal(barrier, inc=1, device_id=(b, z_peer(k)), device_id_type=MESH)

    for copy in small:
        copy.wait()
    for d in range(NB):
        meta[d] = jnp.full((8, T), hub_rows[d] * NB + hub_cols[d], jnp.int32)
    acc[0] = jnp.zeros((T, T), jnp.float32)
    low = factor[...].astype(jnp.bfloat16)
    gath0[b] = low

    pl.semaphore_wait(barrier, NB - 1 + 3 + NZ - 1)

    def pass_on(gath, sweep, block, h, k):
        pltpu.make_async_remote_copy(
            gath.at[block], gath.at[block], ag_ssem.at[sweep], ag_rsem.at[sweep, block],
            device_id=(blk_peer(h, k), g), device_id_type=MESH).start()

    def send_factor(gath, sweep):
        for h, k in ((0, 2), (0, 6), (0, 1), (0, 7), (1, 0)):
            pass_on(gath, sweep, b, h, k)

    def forward_factor(gath, sweep):
        for k, further in ((6, (2, 1)), (2, (7,)), (7, ()), (1, ()), (5, ()), (3, ()), (4, ())):
            block = blk_peer(0, k)
            wait(gath.at[block], ag_rsem.at[sweep, block])
            for f in further:
                pass_on(gath, sweep, block, 0, f)
            pass_on(gath, sweep, block, 1, 0)

    def rest_of_factor(gath, sweep):
        for k in range(NZ):
            block = blk_peer(1, k)
            wait(gath.at[block], ag_rsem.at[sweep, block])

    def gram_start(low, sweep):
        own, into = ((gram_own0, blk_in0), (gram_own1, blk_in1))[sweep]
        own[...] = lax.dot_general(
            low, low, (((0,), (0,)), ((), ())), preferred_element_type=jnp.float32).reshape(NB, 8, T)
        for h, k in BLK_ORDER:
            d = blk_peer(h, k)
            pltpu.make_async_remote_copy(
                own.at[d], into.at[b], gb_ssem.at[sweep], gb_rsem.at[sweep],
                device_id=(d, g), device_id_type=MESH).start()
        into[b] = own[b]

    def gram_quad(sweep):
        into, nxt = ((blk_in0, quad_in0), (blk_in1, quad_in1))[sweep]
        wait(into.at[pl.ds(0, NB - 1)], gb_rsem.at[sweep])
        me = lax.rem(g, 4)
        nxt[me] = jnp.sum(into[...], axis=0)
        for k in (2, 1, 3):
            pltpu.make_async_remote_copy(
                nxt.at[me], nxt.at[me], gq_ssem.at[sweep], gq_rsem.at[sweep],
                device_id=(b, quad(k)), device_id_type=MESH).start()

    def gram_z(sweep):
        into, nxt = ((quad_in0, z_in0), (quad_in1, z_in1))[sweep]
        wait(into.at[pl.ds(0, 3)], gq_rsem.at[sweep])
        nxt[z] = jnp.sum(into[...], axis=0)
        for k in RING:
            pltpu.make_async_remote_copy(
                nxt.at[z], nxt.at[z], gz_ssem.at[sweep], gz_rsem.at[sweep],
                device_id=(b, z_peer(k)), device_id_type=MESH).start()

    def gram_blk(sweep):
        into, gram = ((z_in0, gram0), (z_in1, gram1))[sweep]
        wait(into.at[pl.ds(0, NZ - 1)], gz_rsem.at[sweep])
        gram[b] = jnp.sum(into[...], axis=0)
        for h, k in BLK_ORDER:
            pltpu.make_async_remote_copy(
                gram.at[b], gram.at[b], h_ssem.at[sweep], h_rsem.at[sweep],
                device_id=(blk_peer(h, k), g), device_id_type=MESH).start()

    for h, k in BLK_ORDER:
        d = blk_peer(h, k)
        pltpu.make_async_remote_copy(
            meta.at[d], meta_in.at[b], meta_ssem, meta_rsem, device_id=(d, g), device_id_type=MESH).start()
    send_factor(gath0, 0)
    gram_start(low, 0)
    for h, k in BLK_ORDER:
        d = blk_peer(h, k)
        pltpu.make_async_remote_copy(
            hub_hbm.at[d], hub_v.at[b], hub_ssem, hub_rsem, device_id=(d, g), device_id_type=MESH).start()
    meta_in[b] = meta[b]
    forward_factor(gath0, 0)

    lane = lax.broadcasted_iota(jnp.int32, (8, T), 1)
    sub = lax.broadcasted_iota(jnp.int32, (8, T), 0)

    def lay(u, rows):
        return jnp.where(lane == u, own_rows[u], rows)

    rows = lax.fori_loop(0, OWN, lay, jnp.full((8, T), -1, jnp.int32), unroll=8)
    wait(meta_in.at[pl.ds(0, NB - 1)], meta_rsem)
    hub_r = jnp.full((8, T), -1, jnp.int32)
    hub_c = jnp.zeros((8, T), jnp.int32)
    for e in range(NB):
        v = meta_in[e]
        hub_r = jnp.where(lane == e, v // NB, hub_r)
        hub_c = jnp.where(lane == e, lax.rem(v, NB), hub_c)

    def chain(u, state):
        prev_o, prev_h, last = state
        r = own_rows[u]
        prev_o = jnp.where((rows == r) & (lane > u), u + 1, prev_o)
        prev_h = jnp.where(hub_r == r, u + 1, prev_h)
        last = jnp.where(lane == r, u + 1, last)
        return prev_o, prev_h, last

    zeros = jnp.zeros((8, T), jnp.int32)
    prev_o, prev_h, last = lax.fori_loop(0, OWN, chain, (zeros, zeros, zeros), unroll=8)
    for e in range(NB):
        r = meta_in[e] // NB
        prev_h = jnp.where((hub_r == r) & (lane > e), OWN + e + 1, prev_h)
        last = jnp.where(lane == r, OWN + e + 1, last)
    ptr_v[...] = jnp.where(sub == 0, prev_o, jnp.where(sub == 1, prev_h, jnp.where(sub == 2, last, hub_c)))
    ptr_copy = pltpu.make_async_copy(ptr_v, ptr_s, ptr_sem)
    ptr_copy.start()
    ptr_copy.wait()

    def row_sum(zz, hh, cc):
        return acc[ptr_s[2, zz * 4 + hh * 2 + cc]]

    current = factor[...]
    for sweep in range(ITERS):
        gath, recv_a, recv_b, recv_c, gram = (
            (gath0, recv_a0, recv_b0, recv_c0, gram0),
            (gath1, recv_a1, recv_b1, recv_c1, gram1),
        )[sweep]
        if sweep:
            low = current.astype(jnp.bfloat16)
            gath[b] = low
            send_factor(gath, sweep)
            gram_start(low, sweep)
            forward_factor(gath, sweep)
        gram_quad(sweep)
        rest_of_factor(gath, sweep)

        if sweep == 0:
            tiles_copy.wait()

        def own_step(t, _):
            p = jnp.dot(own_v[t], gath[own_cols[t]], preferred_element_type=jnp.float32)
            acc[t + 1] = acc[ptr_s[0, t]] + p
            return 0

        lax.fori_loop(0, OWN // 2, own_step, 0, unroll=6)
        gram_z(sweep)
        lax.fori_loop(OWN // 2, OWN, own_step, 0, unroll=6)

        if sweep == 0:
            hub_copy.wait()
            wait(hub_v.at[pl.ds(0, NB - 1)], hub_rsem)

        def hub_step(t, _):
            p = jnp.dot(hub_v[t], gath[ptr_s[3, t]], preferred_element_type=jnp.float32)
            acc[OWN + t + 1] = acc[ptr_s[1, t]] + p
            return 0

        lax.fori_loop(0, NB, hub_step, 0, unroll=8)

        if sweep:
            wait(send_a, a_ssem)
            wait(send_b, b_ssem)
            wait(send_c.at[pl.ds(0, NZ - 1)], c_ssem)
        for j in range(2):
            hh = lax.rem(xh + 1 + j, 2)

            def lay_a(k, _):
                send_a[j * NZ + k] = row_sum(k, hh, 1 - c).astype(jnp.bfloat16)
                return 0

            lax.fori_loop(0, NZ, lay_a, 0, unroll=4)
            part = pl.ds(j * NZ, NZ)
            pltpu.make_async_remote_copy(
                send_a.at[part], recv_a.at[part], a_ssem, a_rsem.at[sweep, j],
                device_id=(b, g + 1 - 2 * c), device_id_type=MESH).start()
        wait(recv_a.at[pl.ds(0, NZ)], a_rsem.at[sweep, 0])
        for k in RING + (0,):
            zz = lax.rem(z + k, NZ)
            send_b[zz] = (row_sum(zz, 1 - xh, c) + recv_a[zz].astype(jnp.float32)).astype(jnp.bfloat16)
            pltpu.make_async_remote_copy(
                send_b.at[zz], recv_b.at[zz], b_ssem, b_rsem.at[sweep, zz],
                device_id=(b, g + 2 - 4 * xh), device_id_type=MESH).start()
        gram_blk(sweep)
        wait(recv_a.at[pl.ds(NZ, NZ)], a_rsem.at[sweep, 1])
        total = None
        for k in RING + (0,):
            zz = lax.rem(z + k, NZ)
            mine = row_sum(zz, xh, c) + recv_a[NZ + zz].astype(jnp.float32)
            wait(recv_b.at[zz], b_rsem.at[sweep, zz])
            total = mine + recv_b[zz].astype(jnp.float32)
            if k:
                send_c[zz] = total.astype(jnp.bfloat16)
                pltpu.make_async_remote_copy(
                    send_c.at[zz], recv_c.at[z], c_ssem, c_rsem.at[sweep],
                    device_id=(b, zz * 4 + xh * 2 + c), device_id_type=MESH).start()

        wait(gram.at[pl.ds(0, NB - 1)], h_rsem.at[sweep])
        curvature = jnp.dot(current, gram[...].reshape(T, T), precision=lax.Precision.HIGHEST,
                            preferred_element_type=jnp.float32)
        wait(recv_c.at[pl.ds(0, NZ - 1)], c_rsem.at[sweep])
        for k in RING:
            total = total + recv_c[lax.rem(z + k, NZ)].astype(jnp.float32)
        current = current * (1.0 - damping + damping * total / curvature)

    out[...] = current
    wait(meta_in.at[pl.ds(0, NB - 1)], meta_ssem)
    wait(hub_v.at[pl.ds(0, NB - 1)], hub_ssem)
    for sweep in range(ITERS):
        wait(gath0.at[pl.ds(0, NB - 1)], ag_ssem.at[sweep])
        wait(gram0.at[pl.ds(0, NB - 1)], h_ssem.at[sweep])
        wait(gram0.at[pl.ds(0, NB - 1)], gb_ssem.at[sweep])
        wait(quad_in0.at[pl.ds(0, 3)], gq_ssem.at[sweep])
        wait(z_in0.at[pl.ds(0, NZ - 1)], gz_ssem.at[sweep])
    wait(send_a, a_ssem)
    wait(send_b, b_ssem)
    wait(send_c.at[pl.ds(0, NZ - 1)], c_ssem)


def body(own_tiles, own_rows, own_cols, hub_tiles, hub_rows, hub_cols, factor):
    bf, f32, i32 = jnp.bfloat16, jnp.float32, jnp.int32
    V, S, D = pltpu.VMEM, pltpu.SMEM, pltpu.SemaphoreType.DMA
    vmem, hbm = pl.BlockSpec(memory_space=V), pl.BlockSpec(memory_space=pltpu.HBM)
    return pl.pallas_call(
        kernel,
        out_shape=jax.ShapeDtypeStruct((T, T), f32),
        in_specs=[hbm] * 7,
        out_specs=vmem,
        scratch_shapes=[
            S((OWN,), i32), S((OWN,), i32), S((NB,), i32), S((NB,), i32), V((T, T), f32),
            V((OWN, T, T), bf), V((NB, T, T), bf), V((NB, 8, T), i32), V((NB, 8, T), i32),
            V((NB, T, T), bf), V((NB, T, T), bf), V((OWN + NB + 1, T, T), f32), V((8, T), i32), S((8, T), i32),
            V((2 * NZ, T, T), bf), V((NZ, T, T), bf), V((NZ, T, T), bf),
            V((2 * NZ, T, T), bf), V((2 * NZ, T, T), bf), V((NZ, T, T), bf), V((NZ, T, T), bf),
            V((NZ, T, T), bf), V((NZ, T, T), bf),
            V((NB, 8, T), f32), V((NB, 8, T), f32), V((NB, 8, T), f32), V((NB, 8, T), f32), V((4, 8, T), f32), V((4, 8, T), f32),
            V((NZ, 8, T), f32), V((NZ, 8, T), f32), V((NB, 8, T), f32), V((NB, 8, T), f32),
            D((7,)), D, D, D, D, D,
            D((2,)), D((2, NB)), D, D((2, 2)), D, D((2, NZ)), D, D((2,)),
            D((2,)), D((2,)), D((2,)), D((2,)), D((2,)), D((2,)), D((2,)), D((2,)),
        ],
        compiler_params=pltpu.CompilerParams(
            collective_id=1, has_side_effects=True, vmem_limit_bytes=63 << 20),
    )(own_tiles, own_rows, own_cols, hub_tiles.reshape(NB, T, T), hub_rows.reshape(NB), hub_cols.reshape(NB), factor)


def solution(mesh):
    in_specs = (
        P(("blk", "grp"), None, None),
        P(("blk", "grp")),
        P(("blk", "grp")),
        P(("blk", "grp"), None, None, None),
        P(("blk", "grp"), None),
        P(("blk", "grp"), None),
        P(("blk", "grp"), None),
    )
    out_specs = P(("blk", "grp"), None)
    return jax.shard_map(body, mesh=mesh, in_specs=in_specs, out_specs=out_specs, check_vma=False)
```

```python
import jax
import jax.numpy as jnp
from jax import lax
from jax.experimental import pallas as pl
from jax.experimental.pallas import tpu as pltpu
from jax.sharding import PartitionSpec as P

ITERS = 2
T = 128
NB = 16
NG = 32
NZ = 8
OWN = 120
MESH = pl.DeviceIdType.MESH
damping = 0.5

RING = (4, 3, 5, 2, 6, 1, 7)
BLK_ORDER = tuple((h, k) for k in (4, 3, 5, 2, 6, 1, 7) for h in (1, 0)) + ((1, 0),)


def kernel(own_hbm, own_rows_hbm, own_cols_hbm, hub_hbm, hub_rows_hbm, hub_cols_hbm, factor_hbm, out,
           own_rows, own_cols, hub_rows, hub_cols, factor, own_v, hub_v, meta, meta_in, gath0, gath1, acc, ptr_v, ptr_s,
           send_a, send_b, send_c, recv_a0, recv_a1, recv_b0, recv_b1, recv_c0, recv_c1,
           gram_own0, gram_own1, blk_in0, blk_in1, quad_in0, quad_in1, z_in0, z_in1, gram0, gram1,
           local_sem, ptr_sem, meta_ssem, meta_rsem, hub_ssem, hub_rsem,
           ag_ssem, ag_rsem, a_ssem, a_rsem, b_ssem, b_rsem, c_ssem, c_rsem,
           gb_ssem, gb_rsem, gq_ssem, gq_rsem, gz_ssem, gz_rsem, h_ssem, h_rsem):
    b, g = lax.axis_index("blk"), lax.axis_index("grp")
    y = lax.rem(b, NZ)
    half = b // NZ
    c = lax.rem(g, 2)
    xh = lax.rem(g, 4) // 2
    z = g // 4

    def blk_peer(h, k):
        return lax.rem(half + h, 2) * NZ + lax.rem(y + k, NZ)

    def quad(k):
        return g // 4 * 4 + lax.rem(g + k, 4)

    def z_peer(k):
        return lax.rem(g + 4 * k, NG)

    def wait(like, sem):
        pltpu.make_async_copy(like, like, sem).wait()

    small = [
        pltpu.make_async_copy(src, dst, local_sem.at[2 + i])
        for i, (src, dst) in enumerate((
            (factor_hbm, factor), (hub_rows_hbm, hub_rows), (hub_cols_hbm, hub_cols),
            (own_rows_hbm, own_rows), (own_cols_hbm, own_cols)))
    ]
    for copy in small:
        copy.start()
    tiles_copy = pltpu.make_async_copy(own_hbm, own_v, local_sem.at[0])
    tiles_copy.start()
    hub_copy = pltpu.make_async_copy(hub_hbm.at[b], hub_v.at[b], local_sem.at[1])
    hub_copy.start()

    barrier = pltpu.get_barrier_semaphore()
    for h, k in BLK_ORDER:
        pl.semaphore_signal(barrier, inc=1, device_id=(blk_peer(h, k), g), device_id_type=MESH)

    for k in (1, 2, 3):
        pl.semaphore_signal(barrier, inc=1, device_id=(b, quad(k)), device_id_type=MESH)
    for k in RING:
        pl.semaphore_signal(barrier, inc=1, device_id=(b, z_peer(k)), device_id_type=MESH)

    for copy in small:
        copy.wait()
    for d in range(NB):
        meta[d] = jnp.full((8, T), hub_rows[d] * NB + hub_cols[d], jnp.int32)
    acc[0] = jnp.zeros((T, T), jnp.float32)
    low = factor[...].astype(jnp.bfloat16)
    gath0[b] = low

    pl.semaphore_wait(barrier, NB - 1 + 3 + NZ - 1)

    def pass_on(gath, sweep, block, h, k):
        pltpu.make_async_remote_copy(
            gath.at[block], gath.at[block], ag_ssem.at[sweep], ag_rsem.at[sweep, block],
            device_id=(blk_peer(h, k), g), device_id_type=MESH).start()

    def send_factor(gath, sweep):
        for h, k in ((0, 2), (0, 6), (0, 1), (0, 7), (1, 0)):
            pass_on(gath, sweep, b, h, k)

    def forward_factor(gath, sweep):
        for k, further in ((6, (2, 1)), (2, (7,)), (7, ()), (1, ()), (5, ()), (3, ()), (4, ())):
            if k == 5 and sweep == 0:
                send_hub()
            block = blk_peer(0, k)
            wait(gath.at[block], ag_rsem.at[sweep, block])
            for f in further:
                pass_on(gath, sweep, block, 0, f)
            pass_on(gath, sweep, block, 1, 0)

    def rest_of_factor(gath, sweep):
        for k in range(NZ):
            block = blk_peer(1, k)
            wait(gath.at[block], ag_rsem.at[sweep, block])

    def send_hub():
        for h, k in BLK_ORDER:
            d = blk_peer(h, k)
            pltpu.make_async_remote_copy(
                hub_hbm.at[d], hub_v.at[b], hub_ssem, hub_rsem, device_id=(d, g), device_id_type=MESH).start()

    def gram_start(low, sweep):
        own, into = ((gram_own0, blk_in0), (gram_own1, blk_in1))[sweep]
        own[...] = lax.dot_general(
            low, low, (((0,), (0,)), ((), ())), preferred_element_type=jnp.float32).reshape(NB, 8, T)
        for h, k in BLK_ORDER:
            d = blk_peer(h, k)
            pltpu.make_async_remote_copy(
                own.at[d], into.at[b], gb_ssem.at[sweep], gb_rsem.at[sweep],
                device_id=(d, g), device_id_type=MESH).start()
        into[b] = own[b]

    def gram_quad(sweep):
        into, nxt = ((blk_in0, quad_in0), (blk_in1, quad_in1))[sweep]
        wait(into.at[pl.ds(0, NB - 1)], gb_rsem.at[sweep])
        me = lax.rem(g, 4)
        nxt[me] = jnp.sum(into[...], axis=0)
        for k in (2, 1, 3):
            pltpu.make_async_remote_copy(
                nxt.at[me], nxt.at[me], gq_ssem.at[sweep], gq_rsem.at[sweep],
                device_id=(b, quad(k)), device_id_type=MESH).start()

    def gram_z(sweep):
        into, nxt = ((quad_in0, z_in0), (quad_in1, z_in1))[sweep]
        wait(into.at[pl.ds(0, 3)], gq_rsem.at[sweep])
        nxt[z] = jnp.sum(into[...], axis=0)
        for k in RING:
            pltpu.make_async_remote_copy(
                nxt.at[z], nxt.at[z], gz_ssem.at[sweep], gz_rsem.at[sweep],
                device_id=(b, z_peer(k)), device_id_type=MESH).start()

    def gram_blk(sweep):
        into, gram = ((z_in0, gram0), (z_in1, gram1))[sweep]
        wait(into.at[pl.ds(0, NZ - 1)], gz_rsem.at[sweep])
        gram[b] = jnp.sum(into[...], axis=0)
        for h, k in BLK_ORDER:
            pltpu.make_async_remote_copy(
                gram.at[b], gram.at[b], h_ssem.at[sweep], h_rsem.at[sweep],
                device_id=(blk_peer(h, k), g), device_id_type=MESH).start()

    for h, k in BLK_ORDER:
        d = blk_peer(h, k)
        pltpu.make_async_remote_copy(
            meta.at[d], meta_in.at[b], meta_ssem, meta_rsem, device_id=(d, g), device_id_type=MESH).start()
    send_factor(gath0, 0)
    gram_start(low, 0)
    meta_in[b] = meta[b]
    forward_factor(gath0, 0)

    lane = lax.broadcasted_iota(jnp.int32, (8, T), 1)
    sub = lax.broadcasted_iota(jnp.int32, (8, T), 0)

    def lay(u, rows):
        return jnp.where(lane == u, own_rows[u], rows)

    rows = lax.fori_loop(0, OWN, lay, jnp.full((8, T), -1, jnp.int32), unroll=8)
    wait(meta_in.at[pl.ds(0, NB - 1)], meta_rsem)
    hub_r = jnp.full((8, T), -1, jnp.int32)
    hub_c = jnp.zeros((8, T), jnp.int32)
    for e in range(NB):
        v = meta_in[e]
        hub_r = jnp.where(lane == e, v // NB, hub_r)
        hub_c = jnp.where(lane == e, lax.rem(v, NB), hub_c)

    def chain(u, state):
        prev_o, prev_h, last = state
        r = own_rows[u]
        prev_o = jnp.where((rows == r) & (lane > u), u + 1, prev_o)
        prev_h = jnp.where(hub_r == r, u + 1, prev_h)
        last = jnp.where(lane == r, u + 1, last)
        return prev_o, prev_h, last

    zeros = jnp.zeros((8, T), jnp.int32)
    prev_o, prev_h, last = lax.fori_loop(0, OWN, chain, (zeros, zeros, zeros), unroll=8)
    for e in range(NB):
        r = meta_in[e] // NB
        prev_h = jnp.where((hub_r == r) & (lane > e), OWN + e + 1, prev_h)
        last = jnp.where(lane == r, OWN + e + 1, last)
    ptr_v[...] = jnp.where(sub == 0, prev_o, jnp.where(sub == 1, prev_h, jnp.where(sub == 2, last, hub_c)))
    ptr_copy = pltpu.make_async_copy(ptr_v, ptr_s, ptr_sem)
    ptr_copy.start()
    ptr_copy.wait()

    def row_sum(zz, hh, cc):
        return acc[ptr_s[2, zz * 4 + hh * 2 + cc]]

    current = factor[...]
    for sweep in range(ITERS):
        gath, recv_a, recv_b, recv_c, gram = (
            (gath0, recv_a0, recv_b0, recv_c0, gram0),
            (gath1, recv_a1, recv_b1, recv_c1, gram1),
        )[sweep]
        if sweep:
            low = current.astype(jnp.bfloat16)
            gath[b] = low
            send_factor(gath, sweep)
            gram_start(low, sweep)
            forward_factor(gath, sweep)
        gram_quad(sweep)
        rest_of_factor(gath, sweep)
        gram_z(sweep)

        if sweep == 0:
            tiles_copy.wait()

        def own_step(t, _):
            p = jnp.dot(own_v[t], gath[own_cols[t]], preferred_element_type=jnp.float32)
            acc[t + 1] = acc[ptr_s[0, t]] + p
            return 0

        lax.fori_loop(0, OWN, own_step, 0, unroll=30)

        if sweep == 0:
            hub_copy.wait()
            wait(hub_v.at[pl.ds(0, NB - 1)], hub_rsem)

        def hub_step(t, _):
            p = jnp.dot(hub_v[t], gath[ptr_s[3, t]], preferred_element_type=jnp.float32)
            acc[OWN + t + 1] = acc[ptr_s[1, t]] + p
            return 0

        lax.fori_loop(0, NB, hub_step, 0, unroll=16)

        if sweep:
            wait(send_a, a_ssem)
            wait(send_b, b_ssem)
            wait(send_c.at[pl.ds(0, NZ - 1)], c_ssem)
        for j in range(2):
            hh = lax.rem(xh + 1 + j, 2)

            def lay_a(k, _):
                send_a[j * NZ + k] = row_sum(k, hh, 1 - c).astype(jnp.bfloat16)
                return 0

            lax.fori_loop(0, NZ, lay_a, 0, unroll=4)
            part = pl.ds(j * NZ, NZ)
            pltpu.make_async_remote_copy(
                send_a.at[part], recv_a.at[part], a_ssem, a_rsem.at[sweep, j],
                device_id=(b, g + 1 - 2 * c), device_id_type=MESH).start()
        gram_blk(sweep)
        wait(recv_a.at[pl.ds(0, NZ)], a_rsem.at[sweep, 0])
        for k in RING + (0,):
            zz = lax.rem(z + k, NZ)
            send_b[zz] = (row_sum(zz, 1 - xh, c) + recv_a[zz].astype(jnp.float32)).astype(jnp.bfloat16)
            pltpu.make_async_remote_copy(
                send_b.at[zz], recv_b.at[zz], b_ssem, b_rsem.at[sweep, zz],
                device_id=(b, g + 2 - 4 * xh), device_id_type=MESH).start()
        wait(recv_a.at[pl.ds(NZ, NZ)], a_rsem.at[sweep, 1])
        total = None
        for k in RING + (0,):
            zz = lax.rem(z + k, NZ)
            mine = row_sum(zz, xh, c) + recv_a[NZ + zz].astype(jnp.float32)
            wait(recv_b.at[zz], b_rsem.at[sweep, zz])
            total = mine + recv_b[zz].astype(jnp.float32)
            if k:
                send_c[zz] = total.astype(jnp.bfloat16)
                pltpu.make_async_remote_copy(
                    send_c.at[zz], recv_c.at[z], c_ssem, c_rsem.at[sweep],
                    device_id=(b, zz * 4 + xh * 2 + c), device_id_type=MESH).start()

        wait(gram.at[pl.ds(0, NB - 1)], h_rsem.at[sweep])
        curvature = jnp.dot(current, gram[...].reshape(T, T), precision=lax.Precision.HIGHEST,
                            preferred_element_type=jnp.float32)
        wait(recv_c.at[pl.ds(0, NZ - 1)], c_rsem.at[sweep])
        for k in RING:
            total = total + recv_c[lax.rem(z + k, NZ)].astype(jnp.float32)
        current = current * (1.0 - damping + damping * total / curvature)

    out[...] = current
    wait(meta_in.at[pl.ds(0, NB - 1)], meta_ssem)
    wait(hub_v.at[pl.ds(0, NB - 1)], hub_ssem)
    for sweep in range(ITERS):
        wait(gath0.at[pl.ds(0, NB - 1)], ag_ssem.at[sweep])
        wait(gram0.at[pl.ds(0, NB - 1)], h_ssem.at[sweep])
        wait(gram0.at[pl.ds(0, NB - 1)], gb_ssem.at[sweep])
        wait(quad_in0.at[pl.ds(0, 3)], gq_ssem.at[sweep])
        wait(z_in0.at[pl.ds(0, NZ - 1)], gz_ssem.at[sweep])
    wait(send_a, a_ssem)
    wait(send_b, b_ssem)
    wait(send_c.at[pl.ds(0, NZ - 1)], c_ssem)


def body(own_tiles, own_rows, own_cols, hub_tiles, hub_rows, hub_cols, factor):
    bf, f32, i32 = jnp.bfloat16, jnp.float32, jnp.int32
    V, S, D = pltpu.VMEM, pltpu.SMEM, pltpu.SemaphoreType.DMA
    vmem, hbm = pl.BlockSpec(memory_space=V), pl.BlockSpec(memory_space=pltpu.HBM)
    return pl.pallas_call(
        kernel,
        out_shape=jax.ShapeDtypeStruct((T, T), f32),
        in_specs=[hbm] * 7,
        out_specs=vmem,
        scratch_shapes=[
            S((OWN,), i32), S((OWN,), i32), S((NB,), i32), S((NB,), i32), V((T, T), f32),
            V((OWN, T, T), bf), V((NB, T, T), bf), V((NB, 8, T), i32), V((NB, 8, T), i32),
            V((NB, T, T), bf), V((NB, T, T), bf), V((OWN + NB + 1, T, T), f32), V((8, T), i32), S((8, T), i32),
            V((2 * NZ, T, T), bf), V((NZ, T, T), bf), V((NZ, T, T), bf),
            V((2 * NZ, T, T), bf), V((2 * NZ, T, T), bf), V((NZ, T, T), bf), V((NZ, T, T), bf),
            V((NZ, T, T), bf), V((NZ, T, T), bf),
            V((NB, 8, T), f32), V((NB, 8, T), f32), V((NB, 8, T), f32), V((NB, 8, T), f32), V((4, 8, T), f32), V((4, 8, T), f32),
            V((NZ, 8, T), f32), V((NZ, 8, T), f32), V((NB, 8, T), f32), V((NB, 8, T), f32),
            D((7,)), D, D, D, D, D,
            D((2,)), D((2, NB)), D, D((2, 2)), D, D((2, NZ)), D, D((2,)),
            D((2,)), D((2,)), D((2,)), D((2,)), D((2,)), D((2,)), D((2,)), D((2,)),
        ],
        compiler_params=pltpu.CompilerParams(
            collective_id=1, has_side_effects=True, vmem_limit_bytes=63 << 20),
    )(own_tiles, own_rows, own_cols, hub_tiles.reshape(NB, T, T), hub_rows.reshape(NB), hub_cols.reshape(NB), factor)


def solution(mesh):
    in_specs = (
        P(("blk", "grp"), None, None),
        P(("blk", "grp")),
        P(("blk", "grp")),
        P(("blk", "grp"), None, None, None),
        P(("blk", "grp"), None),
        P(("blk", "grp"), None),
        P(("blk", "grp"), None),
    )
    out_specs = P(("blk", "grp"), None)
    return jax.shard_map(body, mesh=mesh, in_specs=in_specs, out_specs=out_specs, check_vma=False)
```

```python
import jax
import jax.numpy as jnp
from jax import lax
from jax.experimental import pallas as pl
from jax.experimental.pallas import tpu as pltpu
from jax.sharding import PartitionSpec as P

ITERS = 2
T = 128
NB = 16
NG = 32
NZ = 8
OWN = 120
MESH = pl.DeviceIdType.MESH
damping = 0.5

RING = (4, 3, 5, 2, 6, 1, 7)
BLK_ORDER = tuple((h, k) for k in (4, 3, 5, 2, 6, 1, 7) for h in (1, 0)) + ((1, 0),)


def kernel(own_hbm, own_rows_hbm, own_cols_hbm, hub_hbm, hub_rows_hbm, hub_cols_hbm, factor_hbm, out,
           own_rows, own_cols, hub_rows, hub_cols, factor, own_v, hub_v, meta, meta_in, gath0, gath1, acc, ptr_v, ptr_s,
           send_a, send_b, send_c, recv_a0, recv_a1, recv_b0, recv_b1, recv_c0, recv_c1,
           gram_own0, gram_own1, blk_in0, blk_in1, quad_in0, quad_in1, z_in0, z_in1, gram0, gram1,
           local_sem, ptr_sem, meta_ssem, meta_rsem, hub_ssem, hub_rsem,
           ag_ssem, ag_rsem, a_ssem, a_rsem, b_ssem, b_rsem, c_ssem, c_rsem,
           gb_ssem, gb_rsem, gq_ssem, gq_rsem, gz_ssem, gz_rsem, h_ssem, h_rsem):
    b, g = lax.axis_index("blk"), lax.axis_index("grp")
    y = lax.rem(b, NZ)
    half = b // NZ
    c = lax.rem(g, 2)
    xh = lax.rem(g, 4) // 2
    z = g // 4

    def blk_peer(h, k):
        return lax.rem(half + h, 2) * NZ + lax.rem(y + k, NZ)

    def quad(k):
        return g // 4 * 4 + lax.rem(g + k, 4)

    def z_peer(k):
        return lax.rem(g + 4 * k, NG)

    def wait(like, sem):
        pltpu.make_async_copy(like, like, sem).wait()

    small = [
        pltpu.make_async_copy(src, dst, local_sem.at[2 + i])
        for i, (src, dst) in enumerate((
            (factor_hbm, factor), (hub_rows_hbm, hub_rows), (hub_cols_hbm, hub_cols),
            (own_rows_hbm, own_rows), (own_cols_hbm, own_cols)))
    ]
    for copy in small:
        copy.start()
    tiles_copy = pltpu.make_async_copy(own_hbm, own_v, local_sem.at[0])
    tiles_copy.start()
    hub_copy = pltpu.make_async_copy(hub_hbm.at[b], hub_v.at[b], local_sem.at[1])
    hub_copy.start()

    barrier = pltpu.get_barrier_semaphore()
    for h, k in BLK_ORDER:
        pl.semaphore_signal(barrier, inc=1, device_id=(blk_peer(h, k), g), device_id_type=MESH)

    for k in (1, 2, 3):
        pl.semaphore_signal(barrier, inc=1, device_id=(b, quad(k)), device_id_type=MESH)
    for k in RING:
        pl.semaphore_signal(barrier, inc=1, device_id=(b, z_peer(k)), device_id_type=MESH)

    for copy in small:
        copy.wait()
    for d in range(NB):
        meta[d] = jnp.full((8, T), hub_rows[d] * NB + hub_cols[d], jnp.int32)
    acc[0] = jnp.zeros((T, T), jnp.float32)
    low = factor[...].astype(jnp.bfloat16)
    gath0[b] = low

    pl.semaphore_wait(barrier, NB - 1 + 3 + NZ - 1)

    def pass_on(gath, sweep, block, h, k):
        pltpu.make_async_remote_copy(
            gath.at[block], gath.at[block], ag_ssem.at[sweep], ag_rsem.at[sweep, block],
            device_id=(blk_peer(h, k), g), device_id_type=MESH).start()

    def send_factor(gath, sweep):
        for h, k in ((0, 2), (0, 6), (0, 1), (0, 7), (1, 0)):
            pass_on(gath, sweep, b, h, k)

    def forward_factor(gath, sweep):
        for k, further in ((6, (2, 1)), (2, (7,)), (7, ()), (1, ()), (5, ()), (3, ()), (4, ())):
            if k == 1 and sweep == 0:
                send_hub()
            if k == 5 and sweep:
                gram_quad(sweep)
            block = blk_peer(0, k)
            wait(gath.at[block], ag_rsem.at[sweep, block])
            for f in further:
                pass_on(gath, sweep, block, 0, f)
            pass_on(gath, sweep, block, 1, 0)

    def rest_of_factor(gath, sweep):
        for k in (0, 1, 7, 2, 6, 5, 3, 4):
            if k == 5:
                gram_z(sweep)
            block = blk_peer(1, k)
            wait(gath.at[block], ag_rsem.at[sweep, block])

    def send_hub():
        for h, k in BLK_ORDER:
            d = blk_peer(h, k)
            pltpu.make_async_remote_copy(
                hub_hbm.at[d], hub_v.at[b], hub_ssem, hub_rsem, device_id=(d, g), device_id_type=MESH).start()

    def gram_start(low, sweep):
        own, into = ((gram_own0, blk_in0), (gram_own1, blk_in1))[sweep]
        own[...] = lax.dot_general(
            low, low, (((0,), (0,)), ((), ())), preferred_element_type=jnp.float32).reshape(NB, 8, T)
        for h, k in BLK_ORDER:
            d = blk_peer(h, k)
            pltpu.make_async_remote_copy(
                own.at[d], into.at[b], gb_ssem.at[sweep], gb_rsem.at[sweep],
                device_id=(d, g), device_id_type=MESH).start()
        into[b] = own[b]

    def gram_quad(sweep):
        into, nxt = ((blk_in0, quad_in0), (blk_in1, quad_in1))[sweep]
        wait(into.at[pl.ds(0, NB - 1)], gb_rsem.at[sweep])
        me = lax.rem(g, 4)
        nxt[me] = jnp.sum(into[...], axis=0)
        for k in (2, 1, 3):
            pltpu.make_async_remote_copy(
                nxt.at[me], nxt.at[me], gq_ssem.at[sweep], gq_rsem.at[sweep],
                device_id=(b, quad(k)), device_id_type=MESH).start()

    def gram_z(sweep):
        into, nxt = ((quad_in0, z_in0), (quad_in1, z_in1))[sweep]
        wait(into.at[pl.ds(0, 3)], gq_rsem.at[sweep])
        nxt[z] = jnp.sum(into[...], axis=0)
        for k in RING:
            pltpu.make_async_remote_copy(
                nxt.at[z], nxt.at[z], gz_ssem.at[sweep], gz_rsem.at[sweep],
                device_id=(b, z_peer(k)), device_id_type=MESH).start()

    def gram_blk(sweep):
        into, gram = ((z_in0, gram0), (z_in1, gram1))[sweep]
        wait(into.at[pl.ds(0, NZ - 1)], gz_rsem.at[sweep])
        gram[b] = jnp.sum(into[...], axis=0)
        for h, k in BLK_ORDER:
            pltpu.make_async_remote_copy(
                gram.at[b], gram.at[b], h_ssem.at[sweep], h_rsem.at[sweep],
                device_id=(blk_peer(h, k), g), device_id_type=MESH).start()

    for h, k in BLK_ORDER:
        d = blk_peer(h, k)
        pltpu.make_async_remote_copy(
            meta.at[d], meta_in.at[b], meta_ssem, meta_rsem, device_id=(d, g), device_id_type=MESH).start()
    send_factor(gath0, 0)
    gram_start(low, 0)
    meta_in[b] = meta[b]
    forward_factor(gath0, 0)

    lane = lax.broadcasted_iota(jnp.int32, (8, T), 1)
    sub = lax.broadcasted_iota(jnp.int32, (8, T), 0)

    def lay(u, rows):
        return jnp.where(lane == u, own_rows[u], rows)

    rows = lax.fori_loop(0, OWN, lay, jnp.full((8, T), -1, jnp.int32), unroll=8)
    wait(meta_in.at[pl.ds(0, NB - 1)], meta_rsem)
    hub_r = jnp.full((8, T), -1, jnp.int32)
    hub_c = jnp.zeros((8, T), jnp.int32)
    for e in range(NB):
        v = meta_in[e]
        hub_r = jnp.where(lane == e, v // NB, hub_r)
        hub_c = jnp.where(lane == e, lax.rem(v, NB), hub_c)

    def chain(u, state):
        prev_o, prev_h, last = state
        r = own_rows[u]
        prev_o = jnp.where((rows == r) & (lane > u), u + 1, prev_o)
        prev_h = jnp.where(hub_r == r, u + 1, prev_h)
        last = jnp.where(lane == r, u + 1, last)
        return prev_o, prev_h, last

    zeros = jnp.zeros((8, T), jnp.int32)
    prev_o, prev_h, last = lax.fori_loop(0, OWN, chain, (zeros, zeros, zeros), unroll=8)
    for e in range(NB):
        r = meta_in[e] // NB
        prev_h = jnp.where((hub_r == r) & (lane > e), OWN + e + 1, prev_h)
        last = jnp.where(lane == r, OWN + e + 1, last)
    ptr_v[...] = jnp.where(sub == 0, prev_o, jnp.where(sub == 1, prev_h, jnp.where(sub == 2, last, hub_c)))
    ptr_copy = pltpu.make_async_copy(ptr_v, ptr_s, ptr_sem)
    ptr_copy.start()
    ptr_copy.wait()

    def row_sum(zz, hh, cc):
        return acc[ptr_s[2, zz * 4 + hh * 2 + cc]]

    current = factor[...]
    for sweep in range(ITERS):
        gath, recv_a, recv_b, recv_c, gram = (
            (gath0, recv_a0, recv_b0, recv_c0, gram0),
            (gath1, recv_a1, recv_b1, recv_c1, gram1),
        )[sweep]
        if sweep:
            low = current.astype(jnp.bfloat16)
            gath[b] = low
            send_factor(gath, sweep)
            gram_start(low, sweep)
            forward_factor(gath, sweep)
        if sweep == 0:
            gram_quad(sweep)
        rest_of_factor(gath, sweep)

        if sweep == 0:
            tiles_copy.wait()

        def own_step(t, _):
            p = jnp.dot(own_v[t], gath[own_cols[t]], preferred_element_type=jnp.float32)
            acc[t + 1] = acc[ptr_s[0, t]] + p
            return 0

        lax.fori_loop(0, OWN, own_step, 0, unroll=30)

        if sweep == 0:
            hub_copy.wait()
            wait(hub_v.at[pl.ds(0, NB - 1)], hub_rsem)

        def hub_step(t, _):
            p = jnp.dot(hub_v[t], gath[ptr_s[3, t]], preferred_element_type=jnp.float32)
            acc[OWN + t + 1] = acc[ptr_s[1, t]] + p
            return 0

        lax.fori_loop(0, NB, hub_step, 0, unroll=16)

        if sweep:
            wait(send_a, a_ssem)
            wait(send_b, b_ssem)
            wait(send_c.at[pl.ds(0, NZ - 1)], c_ssem)
        for j in range(2):
            hh = lax.rem(xh + 1 + j, 2)

            for k in RING + (0,):
                zz = lax.rem(z + k, NZ)
                at = j * NZ + zz
                send_a[at] = row_sum(zz, hh, 1 - c).astype(jnp.bfloat16)
                pltpu.make_async_remote_copy(
                    send_a.at[at], recv_a.at[at], a_ssem, a_rsem.at[sweep, at],
                    device_id=(b, g + 1 - 2 * c), device_id_type=MESH).start()
        gram_blk(sweep)
        for k in RING + (0,):
            zz = lax.rem(z + k, NZ)
            wait(recv_a.at[zz], a_rsem.at[sweep, zz])
            send_b[zz] = (row_sum(zz, 1 - xh, c) + recv_a[zz].astype(jnp.float32)).astype(jnp.bfloat16)
            pltpu.make_async_remote_copy(
                send_b.at[zz], recv_b.at[zz], b_ssem, b_rsem.at[sweep, zz],
                device_id=(b, g + 2 - 4 * xh), device_id_type=MESH).start()
        total = None
        for k in RING + (0,):
            zz = lax.rem(z + k, NZ)
            wait(recv_a.at[NZ + zz], a_rsem.at[sweep, NZ + zz])
            mine = row_sum(zz, xh, c) + recv_a[NZ + zz].astype(jnp.float32)
            wait(recv_b.at[zz], b_rsem.at[sweep, zz])
            total = mine + recv_b[zz].astype(jnp.float32)
            if k:
                send_c[zz] = total.astype(jnp.bfloat16)
                pltpu.make_async_remote_copy(
                    send_c.at[zz], recv_c.at[z], c_ssem, c_rsem.at[sweep],
                    device_id=(b, zz * 4 + xh * 2 + c), device_id_type=MESH).start()

        wait(gram.at[pl.ds(0, NB - 1)], h_rsem.at[sweep])
        curvature = jnp.dot(current, gram[...].reshape(T, T), precision=lax.Precision.HIGHEST,
                            preferred_element_type=jnp.float32)
        wait(recv_c.at[pl.ds(0, NZ - 1)], c_rsem.at[sweep])
        for k in RING:
            total = total + recv_c[lax.rem(z + k, NZ)].astype(jnp.float32)
        current = current * (1.0 - damping + damping * total / curvature)

    out[...] = current
    wait(meta_in.at[pl.ds(0, NB - 1)], meta_ssem)
    wait(hub_v.at[pl.ds(0, NB - 1)], hub_ssem)
    for sweep in range(ITERS):
        wait(gath0.at[pl.ds(0, NB - 1)], ag_ssem.at[sweep])
        wait(gram0.at[pl.ds(0, NB - 1)], h_ssem.at[sweep])
        wait(gram0.at[pl.ds(0, NB - 1)], gb_ssem.at[sweep])
        wait(quad_in0.at[pl.ds(0, 3)], gq_ssem.at[sweep])
        wait(z_in0.at[pl.ds(0, NZ - 1)], gz_ssem.at[sweep])
    wait(send_a, a_ssem)
    wait(send_b, b_ssem)
    wait(send_c.at[pl.ds(0, NZ - 1)], c_ssem)


def body(own_tiles, own_rows, own_cols, hub_tiles, hub_rows, hub_cols, factor):
    bf, f32, i32 = jnp.bfloat16, jnp.float32, jnp.int32
    V, S, D = pltpu.VMEM, pltpu.SMEM, pltpu.SemaphoreType.DMA
    vmem, hbm = pl.BlockSpec(memory_space=V), pl.BlockSpec(memory_space=pltpu.HBM)
    return pl.pallas_call(
        kernel,
        out_shape=jax.ShapeDtypeStruct((T, T), f32),
        in_specs=[hbm] * 7,
        out_specs=vmem,
        scratch_shapes=[
            S((OWN,), i32), S((OWN,), i32), S((NB,), i32), S((NB,), i32), V((T, T), f32),
            V((OWN, T, T), bf), V((NB, T, T), bf), V((NB, 8, T), i32), V((NB, 8, T), i32),
            V((NB, T, T), bf), V((NB, T, T), bf), V((OWN + NB + 1, T, T), f32), V((8, T), i32), S((8, T), i32),
            V((2 * NZ, T, T), bf), V((NZ, T, T), bf), V((NZ, T, T), bf),
            V((2 * NZ, T, T), bf), V((2 * NZ, T, T), bf), V((NZ, T, T), bf), V((NZ, T, T), bf),
            V((NZ, T, T), bf), V((NZ, T, T), bf),
            V((NB, 8, T), f32), V((NB, 8, T), f32), V((NB, 8, T), f32), V((NB, 8, T), f32), V((4, 8, T), f32), V((4, 8, T), f32),
            V((NZ, 8, T), f32), V((NZ, 8, T), f32), V((NB, 8, T), f32), V((NB, 8, T), f32),
            D((7,)), D, D, D, D, D,
            D((2,)), D((2, NB)), D, D((2, 2 * NZ)), D, D((2, NZ)), D, D((2,)),
            D((2,)), D((2,)), D((2,)), D((2,)), D((2,)), D((2,)), D((2,)), D((2,)),
        ],
        compiler_params=pltpu.CompilerParams(
            collective_id=1, has_side_effects=True, vmem_limit_bytes=63 << 20),
    )(own_tiles, own_rows, own_cols, hub_tiles.reshape(NB, T, T), hub_rows.reshape(NB), hub_cols.reshape(NB), factor)


def solution(mesh):
    in_specs = (
        P(("blk", "grp"), None, None),
        P(("blk", "grp")),
        P(("blk", "grp")),
        P(("blk", "grp"), None, None, None),
        P(("blk", "grp"), None),
        P(("blk", "grp"), None),
        P(("blk", "grp"), None),
    )
    out_specs = P(("blk", "grp"), None)
    return jax.shard_map(body, mesh=mesh, in_specs=in_specs, out_specs=out_specs, check_vma=False)
```

```python
import jax
import jax.numpy as jnp
from jax import lax
from jax.experimental import pallas as pl
from jax.experimental.pallas import tpu as pltpu
from jax.sharding import PartitionSpec as P

ITERS = 2
T = 128
NB = 16
NG = 32
NZ = 8
OWN = 120
MESH = pl.DeviceIdType.MESH
damping = 0.5

RING = (4, 3, 5, 2, 6, 1, 7)
BLK_ORDER = tuple((h, k) for k in (4, 3, 5, 2, 6, 1, 7) for h in (1, 0)) + ((1, 0),)


def kernel(own_hbm, own_rows_hbm, own_cols_hbm, hub_hbm, hub_rows_hbm, hub_cols_hbm, factor_hbm, out,
           own_rows, own_cols, hub_rows, hub_cols, factor, own_v, hub_v, meta, meta_in, gath0, gath1, acc, ptr_v, ptr_s,
           send_a, send_b, send_c, recv_a0, recv_a1, recv_b0, recv_b1, recv_c0, recv_c1,
           gram_own0, gram_own1, blk_in0, blk_in1, quad_in0, quad_in1, z_in0, z_in1, gram0, gram1,
           local_sem, ptr_sem, meta_ssem, meta_rsem, hub_ssem, hub_rsem,
           ag_ssem, ag_rsem, a_ssem, a_rsem, b_ssem, b_rsem, c_ssem, c_rsem,
           gb_ssem, gb_rsem, gq_ssem, gq_rsem, gz_ssem, gz_rsem, h_ssem, h_rsem):
    b, g = lax.axis_index("blk"), lax.axis_index("grp")
    y = lax.rem(b, NZ)
    half = b // NZ
    c = lax.rem(g, 2)
    xh = lax.rem(g, 4) // 2
    z = g // 4

    def blk_peer(h, k):
        return lax.rem(half + h, 2) * NZ + lax.rem(y + k, NZ)

    def quad(k):
        return g // 4 * 4 + lax.rem(g + k, 4)

    def z_peer(k):
        return lax.rem(g + 4 * k, NG)

    def wait(like, sem):
        pltpu.make_async_copy(like, like, sem).wait()

    small = [
        pltpu.make_async_copy(src, dst, local_sem.at[2 + i])
        for i, (src, dst) in enumerate((
            (factor_hbm, factor), (hub_rows_hbm, hub_rows), (hub_cols_hbm, hub_cols),
            (own_rows_hbm, own_rows), (own_cols_hbm, own_cols)))
    ]
    for copy in small:
        copy.start()
    tiles_copy = pltpu.make_async_copy(own_hbm, own_v, local_sem.at[0])
    tiles_copy.start()
    hub_copy = pltpu.make_async_copy(hub_hbm.at[b], hub_v.at[b], local_sem.at[1])
    hub_copy.start()

    barrier = pltpu.get_barrier_semaphore()
    for h, k in BLK_ORDER:
        pl.semaphore_signal(barrier, inc=1, device_id=(blk_peer(h, k), g), device_id_type=MESH)

    for k in (1, 2, 3):
        pl.semaphore_signal(barrier, inc=1, device_id=(b, quad(k)), device_id_type=MESH)
    for k in RING:
        pl.semaphore_signal(barrier, inc=1, device_id=(b, z_peer(k)), device_id_type=MESH)

    for copy in small:
        copy.wait()
    for d in range(NB):
        meta[d] = jnp.full((8, T), hub_rows[d] * NB + hub_cols[d], jnp.int32)
    acc[0] = jnp.zeros((T, T), jnp.float32)
    low = factor[...].astype(jnp.bfloat16)
    gath0[b] = low

    pl.semaphore_wait(barrier, NB - 1 + 3 + NZ - 1)

    def pass_on(gath, sweep, block, h, k):
        pltpu.make_async_remote_copy(
            gath.at[block], gath.at[block], ag_ssem.at[sweep], ag_rsem.at[sweep, block],
            device_id=(blk_peer(h, k), g), device_id_type=MESH).start()

    def send_factor(gath, sweep):
        for h, k in ((0, 2), (0, 6), (0, 1), (0, 7), (1, 0)):
            pass_on(gath, sweep, b, h, k)

    def forward_factor(gath, sweep):
        for k, further in ((6, (2, 1)), (2, (7,)), (7, ()), (1, ()), (5, ()), (3, ()), (4, ())):
            if k == 5 and sweep == 0:
                send_hub()
            block = blk_peer(0, k)
            wait(gath.at[block], ag_rsem.at[sweep, block])
            for f in further:
                pass_on(gath, sweep, block, 0, f)
            pass_on(gath, sweep, block, 1, 0)

    def rest_of_factor(gath, sweep):
        for k in (0, 1, 7, 2, 6, 5, 3, 4):
            if k == 5:
                gram_z(sweep)
            block = blk_peer(1, k)
            wait(gath.at[block], ag_rsem.at[sweep, block])

    def send_hub():
        for h, k in BLK_ORDER:
            d = blk_peer(h, k)
            pltpu.make_async_remote_copy(
                hub_hbm.at[d], hub_v.at[b], hub_ssem, hub_rsem, device_id=(d, g), device_id_type=MESH).start()

    def gram_start(low, sweep):
        own, into = ((gram_own0, blk_in0), (gram_own1, blk_in1))[sweep]
        own[...] = lax.dot_general(
            low, low, (((0,), (0,)), ((), ())), preferred_element_type=jnp.float32).reshape(NB, 8, T)
        for h, k in BLK_ORDER:
            d = blk_peer(h, k)
            pltpu.make_async_remote_copy(
                own.at[d], into.at[b], gb_ssem.at[sweep], gb_rsem.at[sweep],
                device_id=(d, g), device_id_type=MESH).start()
        into[b] = own[b]

    def gram_quad(sweep):
        into, nxt = ((blk_in0, quad_in0), (blk_in1, quad_in1))[sweep]
        wait(into.at[pl.ds(0, NB - 1)], gb_rsem.at[sweep])
        me = lax.rem(g, 4)
        nxt[me] = jnp.sum(into[...], axis=0)
        for k in (2, 1, 3):
            pltpu.make_async_remote_copy(
                nxt.at[me], nxt.at[me], gq_ssem.at[sweep], gq_rsem.at[sweep],
                device_id=(b, quad(k)), device_id_type=MESH).start()

    def gram_z(sweep):
        into, nxt = ((quad_in0, z_in0), (quad_in1, z_in1))[sweep]
        wait(into.at[pl.ds(0, 3)], gq_rsem.at[sweep])
        nxt[z] = jnp.sum(into[...], axis=0)
        for k in RING:
            pltpu.make_async_remote_copy(
                nxt.at[z], nxt.at[z], gz_ssem.at[sweep], gz_rsem.at[sweep],
                device_id=(b, z_peer(k)), device_id_type=MESH).start()

    def gram_blk(sweep):
        into, gram = ((z_in0, gram0), (z_in1, gram1))[sweep]
        wait(into.at[pl.ds(0, NZ - 1)], gz_rsem.at[sweep])
        gram[b] = jnp.sum(into[...], axis=0)
        for h, k in BLK_ORDER:
            pltpu.make_async_remote_copy(
                gram.at[b], gram.at[b], h_ssem.at[sweep], h_rsem.at[sweep],
                device_id=(blk_peer(h, k), g), device_id_type=MESH).start()

    for h, k in BLK_ORDER:
        d = blk_peer(h, k)
        pltpu.make_async_remote_copy(
            meta.at[d], meta_in.at[b], meta_ssem, meta_rsem, device_id=(d, g), device_id_type=MESH).start()
    send_factor(gath0, 0)
    gram_start(low, 0)
    meta_in[b] = meta[b]
    forward_factor(gath0, 0)

    lane = lax.broadcasted_iota(jnp.int32, (8, T), 1)
    sub = lax.broadcasted_iota(jnp.int32, (8, T), 0)

    def lay(u, rows):
        return jnp.where(lane == u, own_rows[u], rows)

    rows = lax.fori_loop(0, OWN, lay, jnp.full((8, T), -1, jnp.int32), unroll=8)
    wait(meta_in.at[pl.ds(0, NB - 1)], meta_rsem)
    hub_r = jnp.full((8, T), -1, jnp.int32)
    hub_c = jnp.zeros((8, T), jnp.int32)
    for e in range(NB):
        v = meta_in[e]
        hub_r = jnp.where(lane == e, v // NB, hub_r)
        hub_c = jnp.where(lane == e, lax.rem(v, NB), hub_c)

    def chain(u, state):
        prev_o, prev_h, last = state
        r = own_rows[u]
        prev_o = jnp.where((rows == r) & (lane > u), u + 1, prev_o)
        prev_h = jnp.where(hub_r == r, u + 1, prev_h)
        last = jnp.where(lane == r, u + 1, last)
        return prev_o, prev_h, last

    zeros = jnp.zeros((8, T), jnp.int32)
    prev_o, prev_h, last = lax.fori_loop(0, OWN, chain, (zeros, zeros, zeros), unroll=8)
    for e in range(NB):
        r = meta_in[e] // NB
        prev_h = jnp.where((hub_r == r) & (lane > e), OWN + e + 1, prev_h)
        last = jnp.where(lane == r, OWN + e + 1, last)
    ptr_v[...] = jnp.where(sub == 0, prev_o, jnp.where(sub == 1, prev_h, jnp.where(sub == 2, last, hub_c)))
    ptr_copy = pltpu.make_async_copy(ptr_v, ptr_s, ptr_sem)
    ptr_copy.start()
    ptr_copy.wait()

    def row_sum(zz, hh, cc):
        return acc[ptr_s[2, zz * 4 + hh * 2 + cc]]

    current = factor[...]
    for sweep in range(ITERS):
        gath, recv_a, recv_b, recv_c, gram = (
            (gath0, recv_a0, recv_b0, recv_c0, gram0),
            (gath1, recv_a1, recv_b1, recv_c1, gram1),
        )[sweep]
        if sweep:
            low = current.astype(jnp.bfloat16)
            gath[b] = low
            send_factor(gath, sweep)
            gram_start(low, sweep)
            forward_factor(gath, sweep)
        gram_quad(sweep)
        rest_of_factor(gath, sweep)

        if sweep == 0:
            tiles_copy.wait()

        def own_step(t, _):
            p = jnp.dot(own_v[t], gath[own_cols[t]], preferred_element_type=jnp.float32)
            acc[t + 1] = acc[ptr_s[0, t]] + p
            return 0

        lax.fori_loop(0, OWN, own_step, 0, unroll=30)

        if sweep == 0:
            hub_copy.wait()
            wait(hub_v.at[pl.ds(0, NB - 1)], hub_rsem)

        def hub_step(t, _):
            p = jnp.dot(hub_v[t], gath[ptr_s[3, t]], preferred_element_type=jnp.float32)
            acc[OWN + t + 1] = acc[ptr_s[1, t]] + p
            return 0

        lax.fori_loop(0, NB, hub_step, 0, unroll=16)

        if sweep:
            wait(send_a, a_ssem)
            wait(send_b, b_ssem)
            wait(send_c.at[pl.ds(0, NZ - 1)], c_ssem)
        for j in range(2):
            hh = lax.rem(xh + 1 + j, 2)

            def lay_a(k, _):
                send_a[j * NZ + k] = row_sum(k, hh, 1 - c).astype(jnp.bfloat16)
                return 0

            lax.fori_loop(0, NZ, lay_a, 0, unroll=4)
            part = pl.ds(j * NZ, NZ)
            pltpu.make_async_remote_copy(
                send_a.at[part], recv_a.at[part], a_ssem, a_rsem.at[sweep, j],
                device_id=(b, g + 1 - 2 * c), device_id_type=MESH).start()
        wait(recv_a.at[pl.ds(0, NZ)], a_rsem.at[sweep, 0])
        for k in RING + (0,):
            zz = lax.rem(z + k, NZ)
            if k == 6:
                gram_blk(sweep)
            send_b[zz] = (row_sum(zz, 1 - xh, c) + recv_a[zz].astype(jnp.float32)).astype(jnp.bfloat16)
            pltpu.make_async_remote_copy(
                send_b.at[zz], recv_b.at[zz], b_ssem, b_rsem.at[sweep, zz],
                device_id=(b, g + 2 - 4 * xh), device_id_type=MESH).start()
        wait(recv_a.at[pl.ds(NZ, NZ)], a_rsem.at[sweep, 1])
        total = None
        for k in RING + (0,):
            zz = lax.rem(z + k, NZ)
            mine = row_sum(zz, xh, c) + recv_a[NZ + zz].astype(jnp.float32)
            wait(recv_b.at[zz], b_rsem.at[sweep, zz])
            total = mine + recv_b[zz].astype(jnp.float32)
            if k:
                send_c[zz] = total.astype(jnp.bfloat16)
                pltpu.make_async_remote_copy(
                    send_c.at[zz], recv_c.at[z], c_ssem, c_rsem.at[sweep],
                    device_id=(b, zz * 4 + xh * 2 + c), device_id_type=MESH).start()

        wait(gram.at[pl.ds(0, NB - 1)], h_rsem.at[sweep])
        curvature = jnp.dot(current, gram[...].reshape(T, T), precision=lax.Precision.HIGHEST,
                            preferred_element_type=jnp.float32)
        wait(recv_c.at[pl.ds(0, NZ - 1)], c_rsem.at[sweep])
        for k in RING:
            total = total + recv_c[lax.rem(z + k, NZ)].astype(jnp.float32)
        current = current * (1.0 - damping + damping * total / curvature)

    out[...] = current
    wait(meta_in.at[pl.ds(0, NB - 1)], meta_ssem)
    wait(hub_v.at[pl.ds(0, NB - 1)], hub_ssem)
    for sweep in range(ITERS):
        wait(gath0.at[pl.ds(0, NB - 1)], ag_ssem.at[sweep])
        wait(gram0.at[pl.ds(0, NB - 1)], h_ssem.at[sweep])
        wait(gram0.at[pl.ds(0, NB - 1)], gb_ssem.at[sweep])
        wait(quad_in0.at[pl.ds(0, 3)], gq_ssem.at[sweep])
        wait(z_in0.at[pl.ds(0, NZ - 1)], gz_ssem.at[sweep])
    wait(send_a, a_ssem)
    wait(send_b, b_ssem)
    wait(send_c.at[pl.ds(0, NZ - 1)], c_ssem)


def body(own_tiles, own_rows, own_cols, hub_tiles, hub_rows, hub_cols, factor):
    bf, f32, i32 = jnp.bfloat16, jnp.float32, jnp.int32
    V, S, D = pltpu.VMEM, pltpu.SMEM, pltpu.SemaphoreType.DMA
    vmem, hbm = pl.BlockSpec(memory_space=V), pl.BlockSpec(memory_space=pltpu.HBM)
    return pl.pallas_call(
        kernel,
        out_shape=jax.ShapeDtypeStruct((T, T), f32),
        in_specs=[hbm] * 7,
        out_specs=vmem,
        scratch_shapes=[
            S((OWN,), i32), S((OWN,), i32), S((NB,), i32), S((NB,), i32), V((T, T), f32),
            V((OWN, T, T), bf), V((NB, T, T), bf), V((NB, 8, T), i32), V((NB, 8, T), i32),
            V((NB, T, T), bf), V((NB, T, T), bf), V((OWN + NB + 1, T, T), f32), V((8, T), i32), S((8, T), i32),
            V((2 * NZ, T, T), bf), V((NZ, T, T), bf), V((NZ, T, T), bf),
            V((2 * NZ, T, T), bf), V((2 * NZ, T, T), bf), V((NZ, T, T), bf), V((NZ, T, T), bf),
            V((NZ, T, T), bf), V((NZ, T, T), bf),
            V((NB, 8, T), f32), V((NB, 8, T), f32), V((NB, 8, T), f32), V((NB, 8, T), f32), V((4, 8, T), f32), V((4, 8, T), f32),
            V((NZ, 8, T), f32), V((NZ, 8, T), f32), V((NB, 8, T), f32), V((NB, 8, T), f32),
            D((7,)), D, D, D, D, D,
            D((2,)), D((2, NB)), D, D((2, 2)), D, D((2, NZ)), D, D((2,)),
            D((2,)), D((2,)), D((2,)), D((2,)), D((2,)), D((2,)), D((2,)), D((2,)),
        ],
        compiler_params=pltpu.CompilerParams(
            collective_id=1, has_side_effects=True, vmem_limit_bytes=63 << 20),
    )(own_tiles, own_rows, own_cols, hub_tiles.reshape(NB, T, T), hub_rows.reshape(NB), hub_cols.reshape(NB), factor)


def solution(mesh):
    in_specs = (
        P(("blk", "grp"), None, None),
        P(("blk", "grp")),
        P(("blk", "grp")),
        P(("blk", "grp"), None, None, None),
        P(("blk", "grp"), None),
        P(("blk", "grp"), None),
        P(("blk", "grp"), None),
    )
    out_specs = P(("blk", "grp"), None)
    return jax.shard_map(body, mesh=mesh, in_specs=in_specs, out_specs=out_specs, check_vma=False)
```
